32 devices in a mesh: dp: 8 (over z, y), expert: 4 (over x, core).
Axes of the slice: x: 2, y: 2, z: 4, core: 2. Of those that a mesh axis runs over, the one named last changes fastest.
Arguments:
- tokens: bfloat16 [4096, 2048], P(('dp', 'expert')), may hold values from -6 to 6
- routes: int32 [4096, 4], P(('dp', 'expert')), may hold values from 0 to 7, all different within a row; in each aligned block of 128 rows (0 to 127, 128 to 255, ...) at most 96 rows name the same one
- combine: bfloat16 [4096, 4], P(('dp', 'expert')), may hold values from 0.049804688 to 1
- out_cotangent: bfloat16 [4096, 2048], P(('dp', 'expert')), may hold values from -1.5 to 1.5
- gate_weight: bfloat16 [8, 2048, 384], P('expert'), may hold values from -0.125 to 0.125
- up_weight: bfloat16 [8, 2048, 384], P('expert'), may hold values from -0.125 to 0.125
- down_weight: bfloat16 [8, 2048, 384], P('expert'), may hold values from -0.3125 to 0.3125
Outputs:
- token_grads: bfloat16 [4096, 2048], P(('dp', 'expert'))
- combine_grads: bfloat16 [4096, 4], P(('dp', 'expert'))
- gate_grads: float32 [8, 2048, 384], P('expert', 'dp')
- up_grads: float32 [8, 2048, 384], P('expert', 'dp')
- down_grads: float32 [8, 2048, 384], P('expert', 'dp')
The draws below stay inside these ranges and needn't reach their ends.
Inputs may be any that keep to these rules, and one draw needn't show every extreme that they name: `routes`: each token names 4 different experts; among the 128 tokens of one device no expert is named more than 96 times, and in some devices an expert is named exactly 96 times.
All inputs are finite; a program needn't handle non-finite values.
Results may differ from the reference program's by a relative error of at most 0.017.
Values may be sent and summed in bfloat16 or wider, within the bound.
A program may use at most 128 MiB of HBM per device.

```python
import math
import jax
import jax.numpy as jnp
import numpy as np
from jax import lax

D = 2048
FF = 384
TOP = 4
TOK_DEV = 128
EXPERTS = 8
CAP = 96
TOKENS = 4096
N_DP = 8
N_EXPERT = 4


def spiked(entries, own_key, source, target, parts, factor):
    owner, partner = [(jnp.arange(entries.shape[axis_at]) // (entries.shape[axis_at] // parts)).reshape([-1 if axis == axis_at else 1 for axis in range(entries.ndim)]) for axis_at in (source, target)]
    chosen = jax.random.permutation(own_key, parts)[partner]
    strong = (owner == chosen) | (owner == (partner + parts // 2) % parts)
    return jnp.where(strong, factor * entries, entries)


def level_of(stream_key, shape, split, smallest, largest):
    def one(dim, parts):
        heights = jax.random.uniform(jax.random.fold_in(jax.random.fold_in(stream_key, 6), dim), (parts,), jnp.float32, smallest / len(split), largest / len(split))
        return jnp.repeat(jnp.exp(heights), shape[dim] // parts).reshape((-1,) + (1,) * (len(shape) - dim - 1))

    level = one(*split[0])
    for cut in split[1:]:
        level = level * one(*cut)
    return level


def routed_block(rng, own, number, rows, amount, top, limit, skew):
    order = jax.random.permutation(rng, amount)
    packed, ordinary = load_shares(amount, rows * top, limit, skew, True), load_shares(amount, rows * top, limit, skew, False)
    places = jnp.arange(amount)

    def named(tallies, rotation):
        used = int((tallies > 0).sum())
        fixed = max(1, used // 4)
        passed = fixed + (places - fixed + rotation * (used - fixed)) % max(1, amount - fixed)
        return jnp.zeros((amount,), jnp.int32).at[order[jnp.where(places < fixed, places, passed)]].set(jnp.asarray(tallies, jnp.int32))

    tallies = jnp.where(number % 4 == 0, named(packed, number // 4), named(ordinary, number - number // 4 - 1))
    mixed = jax.random.permutation(jax.random.fold_in(own, 3), amount)
    source_of, taker = mixed[0:amount // 2 * 2:2], mixed[1:amount // 2 * 2:2]
    slack = jnp.minimum(tallies[source_of] - 1, limit - tallies[taker]) // 2
    slack = jnp.where((source_of == order[0]) | (taker == order[0]) | (tallies[taker] == 0), 0, jnp.maximum(slack, 0))
    passed = jax.random.randint(jax.random.fold_in(own, 4), (amount // 2,), 0, 1 << 20) % (slack + 1)
    tallies = tallies.at[source_of].add(-passed).at[taker].add(passed)
    labels = jnp.searchsorted(jnp.cumsum(tallies), jnp.arange(rows * top), side="right").astype(jnp.int32)
    table = labels.reshape(top, rows).T
    table = table[jax.random.permutation(jax.random.fold_in(own, 1), rows)]
    rotation = jax.random.randint(jax.random.fold_in(own, 2), (rows, 1), 0, top)
    return jnp.take_along_axis(table, (jnp.arange(top)[None, :] + rotation) % top, axis=1)


def load_shares(count, total, bound, slope, full):
    portions = [(1 << 20) // math.isqrt(grade ** slope) + 1 for grade in range(1, count + 1)]
    largest = bound if full else min(bound, max(-(-total // count), total * portions[0] // sum(portions)))
    least = 1 if total - largest >= count - 1 else 0
    given, spare = [largest] + [least] * (count - 1), total - largest - least * (count - 1)
    while spare > 0:
        free = [i for i in range(1, count) if given[i] < largest] or [i for i in range(1, count) if given[i] < bound]
        whole, budget = sum([portions[i] for i in free]), spare
        for i in free:
            addition = min(bound - given[i], max(1, budget * portions[i] // whole), spare)
            given[i] = given[i] + addition
            spare = spare - addition
    return np.array(given)


def gaussian(own_key, extent, scale, reach, cuts=(), kind=jnp.bfloat16):
    entries = scale * jax.random.normal(own_key, extent, jnp.float32)
    if cuts:
        entries = entries * level_of(own_key, extent, cuts, -0.22, 0.18)
    return jnp.clip(entries, -reach, reach).astype(kind)


def bell_draw_with(rng, dims, scale, bound, pieces, heavy, kind=jnp.bfloat16):
    array = scale * jax.random.normal(rng, dims, jnp.float32)
    if pieces:
        array = array * level_of(rng, dims, pieces, -0.22, 0.18)
    return jnp.clip(spiked(array, jax.random.fold_in(rng, 3), *heavy), -bound, bound).astype(kind)


def setup_inputs(seed: int = 0) -> dict:
    splits = jax.random.split(jax.random.key(seed), 8)
    tokens = bell_draw_with(splits[0], (TOKENS, D), 1.0, 6.0, ((0, 32),), (0, 1, 32, 2.75))
    routes_keys = jax.random.split(jax.random.fold_in(splits[1], 1), TOKENS // TOK_DEV)
    routes_turns = jax.random.permutation(jax.random.fold_in(splits[1], 3), TOKENS // TOK_DEV)
    routes = jax.vmap(lambda own, number: routed_block(jax.random.fold_in(splits[1], 2), own, number, TOK_DEV, EXPERTS, TOP, CAP, 2))(routes_keys, routes_turns).reshape((TOKENS, TOP))
    combine = jnp.clip(jnp.exp(math.log(1.0) - 2.9996462 * jax.random.uniform(splits[2], (TOKENS, TOP), jnp.float32) ** level_of(splits[2], (TOKENS, TOP), ((0, 32),), -0.2, 0.2)), 0.049804688, 1.0).astype(jnp.bfloat16)
    out_cotangent = bell_draw_with(splits[3], (TOKENS, D), 0.25, 1.5, ((0, 32),), (0, 1, 32, 2.75))
    gate_weight = gaussian(splits[4], (EXPERTS, D, FF), D ** -0.5, 0.125, ((0, 4),))
    up_weight = gaussian(splits[5], (EXPERTS, D, FF), D ** -0.5, 0.125, ((0, 4),))
    down_weight = gaussian(splits[6], (EXPERTS, D, FF), FF ** -0.5, 0.3125, ((0, 4),))
    return dict(tokens=tokens, routes=routes, combine=combine, out_cotangent=out_cotangent, gate_weight=gate_weight, up_weight=up_weight, down_weight=down_weight)


def build_table(routes):
    devices = N_DP * N_EXPERT
    route_count = TOK_DEV * TOP
    expert_ids = jnp.arange(EXPERTS, dtype=jnp.int32)
    flat_ids = routes.reshape(devices, route_count)
    onehot = (flat_ids[:, :, None] == expert_ids[None, None, :]).astype(jnp.int32)
    before = jnp.cumsum(onehot, axis=1) - onehot
    rank_ids = jnp.sum(before * onehot, axis=2)
    slot_ids = flat_ids * CAP + rank_ids
    source = jnp.arange(devices, dtype=jnp.int32)[:, None] + jnp.zeros((1, route_count), jnp.int32)
    position = source * route_count + jnp.arange(route_count, dtype=jnp.int32)[None, :]
    filled = jnp.full((devices, EXPERTS * CAP), TOKENS * TOP, jnp.int32)
    filled = filled.at[source, slot_ids].set(position)
    return filled.reshape(devices, EXPERTS, CAP)


def group_sum(left, right):
    left_groups = left.astype(jnp.float32).reshape(N_DP, N_EXPERT * CAP, left.shape[1])
    right_groups = right.astype(jnp.float32).reshape(N_DP, N_EXPERT * CAP, right.shape[1])
    partial_sums = jnp.einsum("grd,grf->gdf", left_groups, right_groups).astype(jnp.bfloat16)
    partial_sums = lax.optimization_barrier(partial_sums)
    return jnp.sum(partial_sums.astype(jnp.float32), axis=0)


def reference(tokens, routes, combine, out_cotangent, gate_weight, up_weight, down_weight):
    owners = jnp.transpose(build_table(routes), (1, 0, 2))
    zero_row = jnp.zeros((1, D), jnp.bfloat16)
    token_pad = jnp.concatenate([tokens, zero_row], 0)
    cot_pad = jnp.concatenate([out_cotangent, zero_row], 0)
    weight_pad = jnp.concatenate([combine.reshape(-1), jnp.zeros((1,), jnp.bfloat16)], 0)

    def expert_step(carry, inputs):
        token_acc, score_acc = carry
        owner_ids, gate_w, up_w, down_w = inputs
        owner_ids = owner_ids.reshape(-1)
        row_ids = owner_ids // TOP
        token_rows = token_pad[row_ids]
        gate_act = jnp.dot(token_rows, gate_w, preferred_element_type=jnp.float32)
        up_act = jnp.dot(token_rows, up_w, preferred_element_type=jnp.float32)
        gate_sig = jax.nn.sigmoid(gate_act)
        hidden = (gate_act * gate_sig * up_act).astype(jnp.bfloat16)
        expert_out = jnp.dot(hidden, down_w.T, preferred_element_type=jnp.float32).astype(jnp.bfloat16)
        cot_rows = cot_pad[row_ids]
        weight = weight_pad[owner_ids].astype(jnp.float32)
        scores = jnp.sum(cot_rows.astype(jnp.float32) * expert_out.astype(jnp.float32), axis=1)
        out_cot = (weight[:, None] * cot_rows.astype(jnp.float32)).astype(jnp.bfloat16)
        hidden_cot = jnp.dot(out_cot, down_w, preferred_element_type=jnp.float32)
        gate_cot = (hidden_cot * up_act * gate_sig * (1.0 + gate_act * (1.0 - gate_sig))).astype(jnp.bfloat16)
        up_cot = (hidden_cot * gate_act * gate_sig).astype(jnp.bfloat16)
        rows_cot = (jnp.dot(gate_cot, gate_w.T, preferred_element_type=jnp.float32)
                    + jnp.dot(up_cot, up_w.T, preferred_element_type=jnp.float32)).astype(jnp.bfloat16)
        gate_part = group_sum(token_rows, gate_cot)
        up_part = group_sum(token_rows, up_cot)
        down_part = group_sum(out_cot, hidden)
        token_acc = token_acc.at[row_ids].add(rows_cot.astype(jnp.float32))
        score_acc = score_acc.at[owner_ids].set(scores)
        return (token_acc, score_acc), (gate_part, up_part, down_part)

    start = (jnp.zeros((TOKENS + 1, D), jnp.float32), jnp.zeros((TOKENS * TOP + 1,), jnp.float32))
    (token_acc, score_acc), (gate_grads, up_grads, down_grads) = lax.scan(
        expert_step, start, (owners, gate_weight, up_weight, down_weight))
    token_grads = token_acc[:TOKENS].astype(jnp.bfloat16)
    combine_grads = score_acc[:TOKENS * TOP].reshape(TOKENS, TOP).astype(jnp.bfloat16)
    return token_grads, combine_grads, gate_grads, up_grads, down_grads
```

```python
import functools

import jax
import jax.numpy as jnp
from jax import lax
from jax.experimental import pallas as pl
from jax.experimental.pallas import tpu as pltpu
from jax.sharding import PartitionSpec as P

MESH = pl.DeviceIdType.MESH
LANES = 128
PARTS = 2


def bit_of(index, bit):
    return (index // (1 << bit)) % 2


def flipped(index, bit):
    return index + (1 << bit) * (1 - 2 * bit_of(index, bit))


def partner_mask(index, mask, bits):
    for bit in range(bits):
        if mask >> bit & 1:
            index = flipped(index, bit)
    return index


def position(owner, order):
    place = 0
    for bit in order:
        place = place * 2 + bit_of(owner, bit)
    return place


class Halving:
    def __init__(self, axis, order, buf, recv, send_sem, recv_sem):
        self.axis, self.order, self.buf, self.recv = axis, order, buf, recv
        self.send_sem, self.recv_sem = send_sem, recv_sem
        self.me = lax.axis_index(axis)
        self.count = 1 << len(order)
        self.copies = []

    def base(self, stage):
        place = 0
        for step in range(stage):
            place = place + bit_of(self.me, self.order[step]) * (self.count >> (step + 1))
        return place

    def start(self, stage):
        size = self.count >> (stage + 1)
        bit = self.order[stage]
        begin = self.base(stage) + (1 - bit_of(self.me, bit)) * size
        offset = self.count - (self.count >> stage)
        copy = pltpu.make_async_remote_copy(
            src_ref=self.buf.at[pl.ds(begin, size)],
            dst_ref=self.recv.at[pl.ds(offset, size)],
            send_sem=self.send_sem.at[stage],
            recv_sem=self.recv_sem.at[stage],
            device_id={self.axis: flipped(self.me, bit)},
            device_id_type=MESH,
        )
        copy.start()
        self.copies.append(copy)

    def received(self, stage):
        self.copies[stage].wait_recv()
        size = self.count >> (stage + 1)
        begin = self.base(stage + 1)
        offset = self.count - (self.count >> stage)
        kept = self.buf[pl.ds(begin, size)].astype(jnp.float32)
        return begin, size, kept + self.recv[pl.ds(offset, size)].astype(jnp.float32)

    def step(self, stage):
        begin, size, total = self.received(stage)
        if stage == len(self.order) - 1:
            return total[0]
        self.buf[pl.ds(begin, size)] = total.astype(jnp.bfloat16)
        self.start(stage + 1)
        return None

    def finish(self):
        for copy in self.copies:
            copy.wait_send()


def contract(left, right, dims):
    return lax.dot_general(left, right, (dims, ((), ())), preferred_element_type=jnp.float32)


def kernel(
    ranks, groups,
    tok_hbm, cot_hbm, wd_hbm, gate_hbm, up_hbm, down_hbm,
    tok_out, score_out, gate_out, up_out, down_out,
    x_buf, c_buf, w_buf, weights, cots, parts, parts_recv, score, score_recv,
    local_sem, gather_send, gather_recv, part_send, part_recv,
    tok_send, tok_recv, score_send, score_recv_sem, ready,
):
    rank_bits, group_bits = ranks.bit_length() - 1, groups.bit_length() - 1
    me, group = lax.axis_index("expert"), lax.axis_index("dp")
    experts_here, width, hidden_units = weights.shape[1:]
    rows = x_buf.shape[1]
    owned = width // groups
    part_rows = owned // PARTS

    loads = [
        pltpu.make_async_copy(src, weights.at[i], local_sem.at[i])
        for i, src in enumerate((gate_hbm, up_hbm, down_hbm))
    ]
    own = [
        pltpu.make_async_copy(src, dst.at[me], local_sem.at[3 + i])
        for i, (src, dst) in enumerate(((tok_hbm, x_buf), (cot_hbm, c_buf), (wd_hbm, w_buf)))
    ]
    for copy in own + loads:
        copy.start()

    barrier = pltpu.get_barrier_semaphore()
    for bit in range(rank_bits):
        pl.semaphore_signal(barrier, 1, device_id={"expert": flipped(me, bit)}, device_id_type=MESH)
    for bit in range(group_bits):
        pl.semaphore_signal(barrier, 1, device_id={"dp": flipped(group, bit)}, device_id_type=MESH)
    pl.semaphore_wait(barrier, rank_bits + group_bits)

    gathered = {}

    def send_block(mask, bit, i):
        block = partner_mask(me, mask, rank_bits)
        dst = (x_buf, c_buf, w_buf)[i]
        slot = mask | 1 << bit
        copy = pltpu.make_async_remote_copy(
            src_ref=(tok_hbm, cot_hbm, wd_hbm)[i] if mask == 0 else dst.at[block],
            dst_ref=dst.at[block],
            send_sem=gather_send.at[slot, i],
            recv_sem=gather_recv.at[slot, i],
            device_id={"expert": flipped(me, bit)},
            device_id_type=MESH,
        )
        copy.start()
        gathered[slot, i] = copy

    for i in (2, 0, 1):
        for bit in reversed(range(rank_bits)):
            send_block(0, bit, i)

    lane = lax.broadcasted_iota(jnp.int32, (rows, LANES), 1)

    def forward(block):
        x, c = x_buf[block], c_buf[block]
        route_weights = w_buf[block].astype(jnp.float32)
        scores = jnp.zeros((rows, LANES), jnp.float32)
        for e in range(experts_here):
            mine = lane == me * experts_here + e
            weight = jnp.sum(jnp.where(mine, route_weights, 0.0), axis=1, keepdims=True)
            gate = contract(x, weights[0, e], ((1,), (0,)))
            up = contract(x, weights[1, e], ((1,), (0,)))
            back = contract(c, weights[2, e], ((1,), (0,)))
            sig = jax.nn.sigmoid(gate)
            act = gate * sig
            hidden = (act * up).astype(jnp.bfloat16).astype(jnp.float32)
            scores = jnp.where(mine, jnp.sum(back * hidden, axis=1, keepdims=True), scores)
            back = back * weight
            gate_cot = back * up * sig * (1.0 + gate * (1.0 - sig))
            for kind, value in enumerate((gate_cot, back * act, hidden * weight)):
                at = (kind * experts_here + e) * hidden_units
                cots[block, :, at:at + hidden_units] = value.astype(jnp.bfloat16)
        score[position(block, range(rank_bits))] = scores.astype(jnp.bfloat16)

    for copy in own + loads:
        copy.wait()
    forward(me)
    for mask in range(1, ranks):
        lowest = (mask & -mask).bit_length() - 1
        for i in (2, 0, 1):
            gathered[mask, i].wait_recv()
            for bit in reversed(range(lowest)):
                send_block(mask, bit, i)
        forward(partner_mask(me, mask, rank_bits))
    for copy in gathered.values():
        copy.wait_send()

    first = list(range(group_bits))
    second = [1, 0] + first[2:] if group_bits > 1 else first
    chunks = []

    def weight_grads(kind, source):
        at = kind * experts_here * hidden_units
        orders = [[second if e == 0 and q == 0 else first for q in range(PARTS)]
                  for e in range(experts_here)]

        def one(owner, _):
            columns = pl.ds(pl.multiple_of(owner * owned, LANES), owned)
            left = source[:, :, columns].reshape(ranks * rows, owned)
            right = cots[:, :, at:at + experts_here * hidden_units]
            right = right.reshape(ranks * rows, experts_here * hidden_units)
            total = contract(left, right, ((0,), (0,))).astype(jnp.bfloat16)
            for e in range(experts_here):
                for q in range(PARTS):
                    parts[kind, e, q, position(owner, orders[e][q])] = total[
                        q * part_rows:(q + 1) * part_rows, e * hidden_units:(e + 1) * hidden_units
                    ]
            return 0

        lax.fori_loop(0, groups, one, 0)
        for e in range(experts_here):
            for q in range(PARTS):
                job = Halving(
                    "dp", orders[e][q], parts.at[kind, e, q], parts_recv.at[kind, e, q],
                    part_send.at[kind, e, q], part_recv.at[kind, e, q],
                )
                job.start(0)
                chunks.append((job, kind, e, q))

    weight_grads(2, c_buf)
    for bit in range(rank_bits):
        pl.semaphore_signal(
            ready.at[bit], 1, device_id={"expert": flipped(me, bit)}, device_id_type=MESH
        )
    weight_grads(0, x_buf)
    weight_grads(1, x_buf)

    def token_part(step, _):
        strip = 2 * LANES
        columns = pl.ds(pl.multiple_of(step * strip, LANES), strip)
        total = jnp.zeros((ranks * rows, strip), jnp.float32)
        for kind in range(2):
            for e in range(experts_here):
                at = (kind * experts_here + e) * hidden_units
                left = cots[:, :, at:at + hidden_units].reshape(ranks * rows, hidden_units)
                total += contract(left, weights[kind, e, columns, :], ((1,), (1,)))
        total = total.astype(jnp.bfloat16)
        for r in range(ranks):
            x_buf[position(r, range(rank_bits)), :, columns] = total[r * rows:(r + 1) * rows]
        return 0

    lax.fori_loop(0, width // (2 * LANES), token_part, 0)
    order = list(range(rank_bits))
    token_job = Halving("expert", order, x_buf, c_buf, tok_send, tok_recv)
    score_job = Halving("expert", order, score, score_recv, score_send, score_recv_sem)
    for bit in range(rank_bits):
        pl.semaphore_wait(ready.at[bit], 1)
    token_job.start(0)
    score_job.start(0)

    outs = (gate_out, up_out, down_out)
    for turn in range(len(chunks) + group_bits - 1):
        for stage in range(group_bits):
            if 0 <= turn - stage < len(chunks):
                job, kind, e, q = chunks[turn - stage]
                total = job.step(stage)
                if total is not None:
                    outs[kind][e, q * part_rows:(q + 1) * part_rows, :] = total
        if turn < rank_bits:
            total = token_job.step(turn)
            if total is not None:
                tok_out[...] = total.astype(jnp.bfloat16)
            total = score_job.step(turn)
            if total is not None:
                score_out[...] = total.astype(jnp.bfloat16)
    for job in [chunk[0] for chunk in chunks] + [token_job, score_job]:
        job.finish()


def local(ranks, groups, tokens, routes, combine, out_cotangent, gate_weight, up_weight, down_weight):
    rows, width = tokens.shape
    experts_here, _, hidden_units = gate_weight.shape
    owned = width // groups
    lane = jnp.arange(LANES, dtype=jnp.int32)
    named = routes[:, :, None] == lane
    dense = jnp.sum(jnp.where(named, combine[:, :, None].astype(jnp.float32), 0.0), axis=1)
    dense = dense.astype(jnp.bfloat16)
    rank_bits, group_bits = ranks.bit_length() - 1, groups.bit_length() - 1
    bf16, dma = jnp.bfloat16, pltpu.SemaphoreType.DMA
    anywhere = pl.BlockSpec(memory_space=pl.ANY)
    vmem = pl.BlockSpec(memory_space=pltpu.VMEM)
    grad = jax.ShapeDtypeStruct((experts_here, owned, hidden_units), jnp.float32)
    chunk = (3, experts_here, PARTS)
    block = (owned // PARTS, hidden_units)
    token_grads, scores, gate_grads, up_grads, down_grads = pl.pallas_call(
        functools.partial(kernel, ranks, groups),
        out_shape=(
            jax.ShapeDtypeStruct((rows, width), bf16),
            jax.ShapeDtypeStruct((rows, LANES), bf16),
            grad, grad, grad,
        ),
        in_specs=[anywhere] * 6,
        out_specs=(vmem,) * 5,
        scratch_shapes=[
            pltpu.VMEM((ranks, rows, width), bf16),
            pltpu.VMEM((ranks, rows, width), bf16),
            pltpu.VMEM((ranks, rows, LANES), bf16),
            pltpu.VMEM((3,) + gate_weight.shape, bf16),
            pltpu.VMEM((ranks, rows, 3 * experts_here * hidden_units), bf16),
            pltpu.VMEM(chunk + (groups,) + block, bf16),
            pltpu.VMEM(chunk + (groups - 1,) + block, bf16),
            pltpu.VMEM((ranks, rows, LANES), bf16),
            pltpu.VMEM((ranks, rows, LANES), bf16),
            dma((6,)),
            dma((ranks, 3)),
            dma((ranks, 3)),
            dma(chunk + (group_bits,)),
            dma(chunk + (group_bits,)),
            dma((rank_bits,)),
            dma((rank_bits,)),
            dma((rank_bits,)),
            dma((rank_bits,)),
            pltpu.SemaphoreType.REGULAR((rank_bits,)),
        ],
        compiler_params=pltpu.CompilerParams(
            collective_id=0, has_side_effects=True, vmem_limit_bytes=62 * 2**20
        ),
    )(tokens, out_cotangent, dense, gate_weight, up_weight, down_weight)
    picked = jnp.where(named, scores[:, None, :].astype(jnp.float32), 0.0)
    combine_grads = jnp.sum(picked, axis=2).astype(bf16)
    return token_grads, combine_grads, gate_grads, up_grads, down_grads


def solution(mesh):
    ranks, groups = mesh.shape["expert"], mesh.shape["dp"]
    return jax.shard_map(
        functools.partial(local, ranks, groups),
        mesh=mesh,
        in_specs=(
            P(("dp", "expert"), None),
            P(("dp", "expert"), None),
            P(("dp", "expert"), None),
            P(("dp", "expert"), None),
            P("expert", None, None),
            P("expert", None, None),
            P("expert", None, None),
        ),
        out_specs=(
            P(("dp", "expert"), None),
            P(("dp", "expert"), None),
            P("expert", "dp", None),
            P("expert", "dp", None),
            P("expert", "dp", None),
        ),
        check_vma=False,
    )
```

```python
import functools

import jax
import jax.numpy as jnp
from jax import lax
from jax.experimental import pallas as pl
from jax.experimental.pallas import tpu as pltpu
from jax.sharding import PartitionSpec as P

MESH = pl.DeviceIdType.MESH
LANES = 128
PARTS = 2


def bit_of(index, bit):
    return (index // (1 << bit)) % 2


def flipped(index, bit):
    return index + (1 << bit) * (1 - 2 * bit_of(index, bit))


def partner_mask(index, mask, bits):
    for bit in range(bits):
        if mask >> bit & 1:
            index = flipped(index, bit)
    return index


def position(owner, order):
    place = 0
    for bit in order:
        place = place * 2 + bit_of(owner, bit)
    return place


class Halving:
    def __init__(self, axis, order, buf, recv, send_sem, recv_sem):
        self.axis, self.order, self.buf, self.recv = axis, order, buf, recv
        self.send_sem, self.recv_sem = send_sem, recv_sem
        self.me = lax.axis_index(axis)
        self.count = 1 << len(order)
        self.copies = []

    def base(self, stage):
        place = 0
        for step in range(stage):
            place = place + bit_of(self.me, self.order[step]) * (self.count >> (step + 1))
        return place

    def start(self, stage):
        size = self.count >> (stage + 1)
        bit = self.order[stage]
        begin = self.base(stage) + (1 - bit_of(self.me, bit)) * size
        offset = self.count - (self.count >> stage)
        copy = pltpu.make_async_remote_copy(
            src_ref=self.buf.at[pl.ds(begin, size)],
            dst_ref=self.recv.at[pl.ds(offset, size)],
            send_sem=self.send_sem.at[stage],
            recv_sem=self.recv_sem.at[stage],
            device_id={self.axis: flipped(self.me, bit)},
            device_id_type=MESH,
        )
        copy.start()
        self.copies.append(copy)

    def received(self, stage):
        self.copies[stage].wait_recv()
        size = self.count >> (stage + 1)
        begin = self.base(stage + 1)
        offset = self.count - (self.count >> stage)
        kept = self.buf[pl.ds(begin, size)].astype(jnp.float32)
        return begin, size, kept + self.recv[pl.ds(offset, size)].astype(jnp.float32)

    def step(self, stage):
        begin, size, total = self.received(stage)
        if stage == len(self.order) - 1:
            return total[0]
        self.buf[pl.ds(begin, size)] = total.astype(jnp.bfloat16)
        self.start(stage + 1)
        return None

    def finish(self):
        for copy in self.copies:
            copy.wait_send()


def plan(orders, blocks, links, depth):
    bits = len(orders[0])
    first_link = [links[order[0]] for order in orders]
    free = {link: 0.0 for link in links}
    waiting = {link: [j for j, at in enumerate(first_link) if at == link] for link in links}
    began = {link: [] for link in links}
    ready = []
    events = []
    while ready or any(waiting.values()):
        choices = [(max(free[links[orders[j][s]]], t), 0, t, j, s) for t, j, s in ready]
        choices += [(free[link], 1, 0.0, jobs[0], 0) for link, jobs in waiting.items() if jobs]
        begin, fresh, at, j, s = min(choices)
        link = links[orders[j][s]]
        end = begin + (blocks >> (s + 1))
        free[link] = end
        if fresh:
            waiting[link].pop(0)
            began[link].append(begin)
            back = len(began[link]) - depth
            events.append((began[link][back] if back >= 0 else -1.0, 0, j, 0))
        else:
            ready.remove((at, j, s))
        events.append((end, 1, j, s))
        if s + 1 < bits:
            ready.append((end, j, s + 1))
    return [event[1:] for event in sorted(events)]


def contract(left, right, dims):
    return lax.dot_general(left, right, (dims, ((), ())), preferred_element_type=jnp.float32)


def kernel(
    ranks, groups,
    routes_ref, combine_ref, tok_hbm, cot_hbm, gate_hbm, up_hbm, down_hbm,
    tok_out, score_out, gate_out, up_out, down_out,
    x_buf, c_buf, w_buf, acts, weights, cots, parts, parts_recv, score, score_recv,
    local_sem, gather_send, gather_recv, part_send, part_recv,
    tok_send, tok_recv, score_send, score_recv_sem, ready,
):
    rank_bits, group_bits = ranks.bit_length() - 1, groups.bit_length() - 1
    me, group = lax.axis_index("expert"), lax.axis_index("dp")
    experts_here, width, hidden_units = weights.shape[1:]
    rows = x_buf.shape[1]
    owned = width // groups
    part_rows = owned // PARTS

    loads = [
        pltpu.make_async_copy(src, weights.at[i], local_sem.at[i])
        for i, src in enumerate((gate_hbm, up_hbm, down_hbm))
    ]
    own = [
        pltpu.make_async_copy(src, dst.at[me], local_sem.at[3 + i])
        for i, (src, dst) in enumerate(((tok_hbm, x_buf), (cot_hbm, c_buf)))
    ]
    for copy in own + loads:
        copy.start()

    top = routes_ref.shape[0]
    expert = lax.broadcasted_iota(jnp.int32, (LANES, rows), 0)
    named = [expert == routes_ref[k:k + 1, :] for k in range(top)]
    dense = jnp.zeros((LANES, rows), jnp.float32)
    for k in range(top):
        dense = jnp.where(named[k], combine_ref[k:k + 1, :].astype(jnp.float32), dense)
    w_buf[me] = dense.T.astype(jnp.bfloat16)

    barrier = pltpu.get_barrier_semaphore()
    for bit in range(rank_bits):
        pl.semaphore_signal(barrier, 1, device_id={"expert": flipped(me, bit)}, device_id_type=MESH)
    for bit in range(group_bits):
        pl.semaphore_signal(barrier, 1, device_id={"dp": flipped(group, bit)}, device_id_type=MESH)
    pl.semaphore_wait(barrier, rank_bits + group_bits)

    gathered = {}

    def send_block(mask, bit, i):
        block = partner_mask(me, mask, rank_bits)
        dst = (x_buf, c_buf, w_buf)[i]
        slot = mask | 1 << bit
        copy = pltpu.make_async_remote_copy(
            src_ref=(tok_hbm, cot_hbm)[i] if mask == 0 and i < 2 else dst.at[block],
            dst_ref=dst.at[block],
            send_sem=gather_send.at[slot, i],
            recv_sem=gather_recv.at[slot, i],
            device_id={"expert": flipped(me, bit)},
            device_id_type=MESH,
        )
        copy.start()
        gathered[slot, i] = copy

    for bit in reversed(range(rank_bits)):
        send_block(0, bit, 2)
    for bit in reversed(range(rank_bits)):
        send_block(0, bit, 0)
    send_block(0, 0, 1)

    both = 2 * rows
    lane = lax.broadcasted_iota(jnp.int32, (both, LANES), 1)

    def forward(pair):
        x = x_buf[pl.ds(pair, 2)].reshape(both, width)
        for kind in range(2):
            for e in range(experts_here):
                acts[kind, e] = contract(x, weights[kind, e], ((1,), (0,)))

    def backward(pair):
        c = c_buf[pl.ds(pair, 2)].reshape(both, width)
        route_weights = w_buf[pl.ds(pair, 2)].reshape(both, LANES).astype(jnp.float32)
        scores = jnp.zeros((both, LANES), jnp.float32)
        for e in range(experts_here):
            mine = lane == me * experts_here + e
            weight = jnp.sum(jnp.where(mine, route_weights, 0.0), axis=1, keepdims=True)
            back = contract(c, weights[2, e], ((1,), (0,)))
            gate, up = acts[0, e], acts[1, e]
            sig = jax.nn.sigmoid(gate)
            act = gate * sig
            hidden = (act * up).astype(jnp.bfloat16).astype(jnp.float32)
            scores = jnp.where(mine, jnp.sum(back * hidden, axis=1, keepdims=True), scores)
            back = back * weight
            gate_cot = back * up * sig * (1.0 + gate * (1.0 - sig))
            for kind, value in enumerate((gate_cot, back * act, hidden * weight)):
                at = (kind * experts_here + e) * hidden_units
                value = value.astype(jnp.bfloat16).reshape(2, rows, hidden_units)
                cots[pl.ds(pair, 2), :, at:at + hidden_units] = value
        scores = scores.astype(jnp.bfloat16)
        for i in range(2):
            place = position(pair + i, range(rank_bits))
            score[place] = scores[i * rows:(i + 1) * rows]

    def arrived(mask, i):
        gathered[mask, i].wait_recv()
        lowest = (mask & -mask).bit_length() - 1
        for bit in reversed(range(lowest)):
            send_block(mask, bit, i)

    own_pair = me // 2 * 2
    own[0].wait()
    loads[0].wait()
    loads[1].wait()
    arrived(1, 0)
    forward(own_pair)
    own[1].wait()
    loads[2].wait()
    arrived(1, 1)
    arrived(1, 2)
    backward(own_pair)
    for bit in reversed(range(1, rank_bits)):
        gathered[1 << bit, 0].wait_send()
        send_block(0, bit, 1)
    for mask in range(2, ranks, 2):
        pair = partner_mask(own_pair, mask, rank_bits)
        for i in (2, 0):
            arrived(mask, i)
            arrived(mask + 1, i)
        forward(pair)
        arrived(mask, 1)
        arrived(mask + 1, 1)
        backward(pair)
    early = [(1 << bit, 0) for bit in range(1, rank_bits)]
    for key, copy in gathered.items():
        if key not in early:
            copy.wait_send()

    first = list(range(group_bits))
    second = [1, 0] + first[2:] if group_bits > 1 else first
    second_at = [(e, q) for e in range(experts_here) for q in range(PARTS)][:1]
    chunks = []
    for kind in (2, 0, 1):
        for e in range(experts_here):
            for q in range(PARTS):
                job = Halving(
                    "dp", second if (e, q) in second_at else first,
                    parts.at[kind, e, q], parts_recv.at[kind, e, q],
                    part_send.at[kind, e, q], part_recv.at[kind, e, q],
                )
                chunks.append((job, kind, e, q))
    links = [0 if bit < max(1, group_bits // 2) else 1 for bit in range(group_bits)]
    events = plan([chunk[0].order for chunk in chunks], groups, links, 2)

    def weight_grads(kind, source):
        at = kind * experts_here * hidden_units
        orders = {(e, q): job.order for job, kind_of, e, q in chunks if kind_of == kind}

        def one(owner, _):
            columns = pl.ds(pl.multiple_of(owner * owned, LANES), owned)
            left = source[:, :, columns].reshape(ranks * rows, owned)
            right = cots[:, :, at:at + experts_here * hidden_units]
            right = right.reshape(ranks * rows, experts_here * hidden_units)
            total = contract(left, right, ((0,), (0,))).astype(jnp.bfloat16)
            for e in range(experts_here):
                for q in range(PARTS):
                    parts[kind, e, q, position(owner, orders[e, q])] = total[
                        q * part_rows:(q + 1) * part_rows, e * hidden_units:(e + 1) * hidden_units
                    ]
            return 0

        lax.fori_loop(0, groups, one, 0)
    weight_grads(2, c_buf)
    early = [event for event in events if not event[0]][:3]
    early = [event for event in early if chunks[event[1]][1] == 2]
    for _, j, _ in early:
        chunks[j][0].start(0)
    for bit in range(rank_bits):
        pl.semaphore_signal(
            ready.at[bit], 1, device_id={"expert": flipped(me, bit)}, device_id_type=MESH
        )
    weight_grads(0, x_buf)
    weight_grads(1, x_buf)

    def token_part(step, _):
        strip = 2 * LANES
        columns = pl.ds(pl.multiple_of(step * strip, LANES), strip)
        total = jnp.zeros((ranks * rows, strip), jnp.float32)
        for kind in range(2):
            for e in range(experts_here):
                at = (kind * experts_here + e) * hidden_units
                left = cots[:, :, at:at + hidden_units].reshape(ranks * rows, hidden_units)
                total += contract(left, weights[kind, e, columns, :], ((1,), (1,)))
        total = total.astype(jnp.bfloat16)
        for r in range(ranks):
            x_buf[position(r, range(rank_bits)), :, columns] = total[r * rows:(r + 1) * rows]
        return 0

    lax.fori_loop(0, width // (2 * LANES), token_part, 0)
    order = list(range(rank_bits))
    token_job = Halving("expert", order, x_buf, c_buf, tok_send, tok_recv)
    score_job = Halving("expert", order, score, score_recv, score_send, score_recv_sem)
    for bit in range(rank_bits):
        pl.semaphore_wait(ready.at[bit], 1)
    token_job.start(0)
    score_job.start(0)

    outs = (gate_out, up_out, down_out)
    turn = 0
    for event in events:
        is_step, j, stage = event
        job, kind, e, q = chunks[j]
        if not is_step:
            if event not in early:
                job.start(0)
            continue
        total = job.step(stage)
        if total is not None:
            outs[kind][e, q * part_rows:(q + 1) * part_rows, :] = total.astype(jnp.bfloat16)
        if turn % 4 == 3 and turn // 4 < rank_bits:
            total = token_job.step(turn // 4)
            if total is not None:
                tok_out[...] = total.astype(jnp.bfloat16)
            total = score_job.step(turn // 4)
            if total is not None:
                total = total.T
                for k in range(top):
                    picked = jnp.where(named[k], total, 0.0)
                    grads = jnp.sum(picked, axis=0, keepdims=True)
                    score_out[k:k + 1, :] = grads.astype(jnp.bfloat16)
        turn += 1
    for job in [chunk[0] for chunk in chunks] + [token_job, score_job]:
        job.finish()


def local(ranks, groups, tokens, routes, combine, out_cotangent, gate_weight, up_weight, down_weight):
    rows, width = tokens.shape
    experts_here, _, hidden_units = gate_weight.shape
    owned = width // groups
    rank_bits, group_bits = ranks.bit_length() - 1, groups.bit_length() - 1
    bf16, dma = jnp.bfloat16, pltpu.SemaphoreType.DMA
    anywhere = pl.BlockSpec(memory_space=pl.ANY)
    vmem = pl.BlockSpec(memory_space=pltpu.VMEM)
    grad = jax.ShapeDtypeStruct((experts_here, owned, hidden_units), bf16)
    chunk = (3, experts_here, PARTS)
    block = (owned // PARTS, hidden_units)
    token_grads, scores, gate_grads, up_grads, down_grads = pl.pallas_call(
        functools.partial(kernel, ranks, groups),
        out_shape=(
            jax.ShapeDtypeStruct((rows, width), bf16),
            jax.ShapeDtypeStruct(routes.shape[::-1], bf16),
            grad, grad, grad,
        ),
        in_specs=[vmem] * 2 + [anywhere] * 5,
        out_specs=(vmem,) * 5,
        scratch_shapes=[
            pltpu.VMEM((ranks, rows, width), bf16),
            pltpu.VMEM((ranks, rows, width), bf16),
            pltpu.VMEM((ranks, rows, LANES), bf16),
            pltpu.VMEM((2, experts_here, 2 * rows, hidden_units), jnp.float32),
            pltpu.VMEM((3,) + gate_weight.shape, bf16),
            pltpu.VMEM((ranks, rows, 3 * experts_here * hidden_units), bf16),
            pltpu.VMEM(chunk + (groups,) + block, bf16),
            pltpu.VMEM(chunk + (groups - 1,) + block, bf16),
            pltpu.VMEM((ranks, rows, LANES), bf16),
            pltpu.VMEM((ranks, rows, LANES), bf16),
            dma((5,)),
            dma((ranks, 3)),
            dma((ranks, 3)),
            dma(chunk + (group_bits,)),
            dma(chunk + (group_bits,)),
            dma((rank_bits,)),
            dma((rank_bits,)),
            dma((rank_bits,)),
            dma((rank_bits,)),
            pltpu.SemaphoreType.REGULAR((rank_bits,)),
        ],
        compiler_params=pltpu.CompilerParams(
            collective_id=0, has_side_effects=True, vmem_limit_bytes=62 * 2**20
        ),
    )(routes.T, combine.T, tokens, out_cotangent, gate_weight, up_weight, down_weight)
    weight_grads = tuple(x.astype(jnp.float32) for x in (gate_grads, up_grads, down_grads))
    return (token_grads, scores.T) + weight_grads


def solution(mesh):
    ranks, groups = mesh.shape["expert"], mesh.shape["dp"]
    return jax.shard_map(
        functools.partial(local, ranks, groups),
        mesh=mesh,
        in_specs=(
            P(("dp", "expert"), None),
            P(("dp", "expert"), None),
            P(("dp", "expert"), None),
            P(("dp", "expert"), None),
            P("expert", None, None),
            P("expert", None, None),
            P("expert", None, None),
        ),
        out_specs=(
            P(("dp", "expert"), None),
            P(("dp", "expert"), None),
            P("expert", "dp", None),
            P("expert", "dp", None),
            P("expert", "dp", None),
        ),
        check_vma=False,
    )
```

```python
import functools

import jax
import jax.numpy as jnp
from jax import lax
from jax.experimental import pallas as pl
from jax.experimental.pallas import tpu as pltpu
from jax.sharding import PartitionSpec as P

MESH = pl.DeviceIdType.MESH
LANES = 128
PARTS = 2


def bit_of(index, bit):
    return (index // (1 << bit)) % 2


def flipped(index, bit):
    return index + (1 << bit) * (1 - 2 * bit_of(index, bit))


def partner_mask(index, mask, bits):
    for bit in range(bits):
        if mask >> bit & 1:
            index = flipped(index, bit)
    return index


def position(owner, order):
    place = 0
    for bit in order:
        place = place * 2 + bit_of(owner, bit)
    return place


class Halving:
    def __init__(self, axis, order, buf, recv, send_sem, recv_sem):
        self.axis, self.order, self.buf, self.recv = axis, order, buf, recv
        self.send_sem, self.recv_sem = send_sem, recv_sem
        self.me = lax.axis_index(axis)
        self.count = 1 << len(order)
        self.copies = []

    def base(self, stage):
        place = 0
        for step in range(stage):
            place = place + bit_of(self.me, self.order[step]) * (self.count >> (step + 1))
        return place

    def start(self, stage):
        size = self.count >> (stage + 1)
        bit = self.order[stage]
        begin = self.base(stage) + (1 - bit_of(self.me, bit)) * size
        offset = self.count - (self.count >> stage)
        copy = pltpu.make_async_remote_copy(
            src_ref=self.buf.at[pl.ds(begin, size)],
            dst_ref=self.recv.at[pl.ds(offset, size)],
            send_sem=self.send_sem.at[stage],
            recv_sem=self.recv_sem.at[stage],
            device_id={self.axis: flipped(self.me, bit)},
            device_id_type=MESH,
        )
        copy.start()
        self.copies.append(copy)

    def received(self, stage):
        self.copies[stage].wait_recv()
        size = self.count >> (stage + 1)
        begin = self.base(stage + 1)
        offset = self.count - (self.count >> stage)
        kept = self.buf[pl.ds(begin, size)].astype(jnp.float32)
        return begin, size, kept + self.recv[pl.ds(offset, size)].astype(jnp.float32)

    def step(self, stage):
        begin, size, total = self.received(stage)
        if stage == len(self.order) - 1:
            return total[0]
        self.buf[pl.ds(begin, size)] = total.astype(jnp.bfloat16)
        self.start(stage + 1)
        return None

    def finish(self):
        for copy in self.copies:
            copy.wait_send()


def plan(orders, blocks, links, depth):
    bits = len(orders[0])
    first_link = [links[order[0]] for order in orders]
    free = {link: 0.0 for link in links}
    waiting = {link: [j for j, at in enumerate(first_link) if at == link] for link in links}
    began = {link: [] for link in links}
    ready = []
    events = []
    while ready or any(waiting.values()):
        choices = [(max(free[links[orders[j][s]]], t), 0, t, j, s) for t, j, s in ready]
        choices += [(free[link], 1, 0.0, jobs[0], 0) for link, jobs in waiting.items() if jobs]
        begin, fresh, at, j, s = min(choices)
        link = links[orders[j][s]]
        end = begin + (blocks >> (s + 1))
        free[link] = end
        if fresh:
            waiting[link].pop(0)
            began[link].append(begin)
            back = len(began[link]) - depth
            events.append((began[link][back] if back >= 0 else -1.0, 0, j, 0))
        else:
            ready.remove((at, j, s))
        events.append((end, 1, j, s))
        if s + 1 < bits:
            ready.append((end, j, s + 1))
    return [event[1:] for event in sorted(events)]


def contract(left, right, dims):
    return lax.dot_general(left, right, (dims, ((), ())), preferred_element_type=jnp.float32)


def kernel(
    ranks, groups,
    routes_ref, combine_ref, tok_hbm, cot_hbm, gate_hbm, up_hbm, down_hbm,
    tok_out, score_out, gate_out, up_out, down_out,
    x_buf, c_buf, w_buf, acts, weights, cots, parts, parts_recv, score, score_recv,
    local_sem, gather_send, gather_recv, part_send, part_recv,
    tok_send, tok_recv, score_send, score_recv_sem, ready,
):
    rank_bits, group_bits = ranks.bit_length() - 1, groups.bit_length() - 1
    me, group = lax.axis_index("expert"), lax.axis_index("dp")
    experts_here, width, hidden_units = weights.shape[1:]
    rows = x_buf.shape[1]
    owned = width // groups
    part_rows = owned // PARTS

    loads = [
        pltpu.make_async_copy(src, weights.at[i], local_sem.at[i])
        for i, src in enumerate((gate_hbm, up_hbm, down_hbm))
    ]
    own = [
        pltpu.make_async_copy(src, dst.at[me], local_sem.at[3 + i])
        for i, (src, dst) in enumerate(((tok_hbm, x_buf), (cot_hbm, c_buf)))
    ]
    for copy in own + loads:
        copy.start()

    top = routes_ref.shape[0]
    expert = lax.broadcasted_iota(jnp.int32, (LANES, rows), 0)
    named = [expert == routes_ref[k:k + 1, :] for k in range(top)]
    dense = jnp.zeros((LANES, rows), jnp.float32)
    for k in range(top):
        dense = jnp.where(named[k], combine_ref[k:k + 1, :].astype(jnp.float32), dense)
    w_buf[me] = dense.T.astype(jnp.bfloat16)

    barrier = pltpu.get_barrier_semaphore()
    for bit in range(rank_bits):
        pl.semaphore_signal(barrier, 1, device_id={"expert": flipped(me, bit)}, device_id_type=MESH)
    for bit in range(group_bits):
        pl.semaphore_signal(barrier, 1, device_id={"dp": flipped(group, bit)}, device_id_type=MESH)
    pl.semaphore_wait(barrier, rank_bits + group_bits)

    gathered = {}

    def send_block(mask, bit, i):
        block = partner_mask(me, mask, rank_bits)
        dst = (x_buf, c_buf, w_buf)[i]
        slot = mask | 1 << bit
        copy = pltpu.make_async_remote_copy(
            src_ref=(tok_hbm, cot_hbm)[i] if mask == 0 and i < 2 else dst.at[block],
            dst_ref=dst.at[block],
            send_sem=gather_send.at[slot, i],
            recv_sem=gather_recv.at[slot, i],
            device_id={"expert": flipped(me, bit)},
            device_id_type=MESH,
        )
        copy.start()
        gathered[slot, i] = copy

    for bit in reversed(range(rank_bits)):
        send_block(0, bit, 2)
    for bit in reversed(range(rank_bits)):
        send_block(0, bit, 0)
    send_block(0, 0, 1)

    both = 2 * rows
    lane = lax.broadcasted_iota(jnp.int32, (both, LANES), 1)

    def forward(pair):
        x = x_buf[pl.ds(pair, 2)].reshape(both, width)
        for kind in range(2):
            for e in range(experts_here):
                acts[kind, e] = contract(x, weights[kind, e], ((1,), (0,)))

    def backward(pair):
        c = c_buf[pl.ds(pair, 2)].reshape(both, width)
        route_weights = w_buf[pl.ds(pair, 2)].reshape(both, LANES).astype(jnp.float32)
        scores = jnp.zeros((both, LANES), jnp.float32)
        for e in range(experts_here):
            mine = lane == me * experts_here + e
            weight = jnp.sum(jnp.where(mine, route_weights, 0.0), axis=1, keepdims=True)
            back = contract(c, weights[2, e], ((1,), (0,)))
            gate, up = acts[0, e], acts[1, e]
            sig = jax.nn.sigmoid(gate)
            act = gate * sig
            hidden = (act * up).astype(jnp.bfloat16).astype(jnp.float32)
            scores = jnp.where(mine, jnp.sum(back * hidden, axis=1, keepdims=True), scores)
            back = back * weight
            gate_cot = back * up * sig * (1.0 + gate * (1.0 - sig))
            for kind, value in enumerate((gate_cot, back * act, hidden * weight)):
                at = (kind * experts_here + e) * hidden_units
                value = value.astype(jnp.bfloat16).reshape(2, rows, hidden_units)
                cots[pl.ds(pair, 2), :, at:at + hidden_units] = value
        scores = scores.astype(jnp.bfloat16)
        for i in range(2):
            place = position(pair + i, range(rank_bits))
            score[place] = scores[i * rows:(i + 1) * rows]

    def arrived(mask, i):
        gathered[mask, i].wait_recv()
        lowest = (mask & -mask).bit_length() - 1
        for bit in reversed(range(lowest)):
            send_block(mask, bit, i)

    own_pair = me // 2 * 2
    own[0].wait()
    loads[0].wait()
    loads[1].wait()
    arrived(1, 0)
    forward(own_pair)
    own[1].wait()
    loads[2].wait()
    arrived(1, 1)
    arrived(1, 2)
    backward(own_pair)
    for bit in reversed(range(1, rank_bits)):
        gathered[1 << bit, 0].wait_send()
        send_block(0, bit, 1)
    for mask in range(2, ranks, 2):
        pair = partner_mask(own_pair, mask, rank_bits)
        for i in (2, 0):
            arrived(mask, i)
            arrived(mask + 1, i)
        forward(pair)
        arrived(mask, 1)
        arrived(mask + 1, 1)
        backward(pair)
    early = [(1 << bit, 0) for bit in range(1, rank_bits)]
    for key, copy in gathered.items():
        if key not in early:
            copy.wait_send()

    first = list(range(group_bits))
    second = [1, 0] + first[2:] if group_bits > 1 else first
    second_at = [(e, q) for e in range(experts_here) for q in range(PARTS)][:1]
    chunks = []
    for kind in (2, 0, 1):
        for e in range(experts_here):
            for q in range(PARTS):
                job = Halving(
                    "dp", second if (e, q) in second_at else first,
                    parts.at[kind, e, q], parts_recv.at[kind, e, q],
                    part_send.at[kind, e, q], part_recv.at[kind, e, q],
                )
                chunks.append((job, kind, e, q))
    links = [0 if bit < max(1, group_bits // 2) else 1 for bit in range(group_bits)]
    events = plan([chunk[0].order for chunk in chunks], groups, links, 3)

    def weight_grads(kind, source):
        at = kind * experts_here * hidden_units
        orders = {(e, q): job.order for job, kind_of, e, q in chunks if kind_of == kind}

        def one(owner, _):
            columns = pl.ds(pl.multiple_of(owner * owned, LANES), owned)
            left = source[:, :, columns].reshape(ranks * rows, owned)
            right = cots[:, :, at:at + experts_here * hidden_units]
            right = right.reshape(ranks * rows, experts_here * hidden_units)
            total = contract(left, right, ((0,), (0,))).astype(jnp.bfloat16)
            for e in range(experts_here):
                for q in range(PARTS):
                    parts[kind, e, q, position(owner, orders[e, q])] = total[
                        q * part_rows:(q + 1) * part_rows, e * hidden_units:(e + 1) * hidden_units
                    ]
            return 0

        lax.fori_loop(0, groups, one, 0)
    weight_grads(2, c_buf)
    for bit in range(rank_bits):
        pl.semaphore_signal(
            ready.at[bit], 1, device_id={"expert": flipped(me, bit)}, device_id_type=MESH
        )

    def token_part(step, _):
        strip = 2 * LANES
        columns = pl.ds(pl.multiple_of(step * strip, LANES), strip)
        total = jnp.zeros((ranks * rows, strip), jnp.float32)
        for kind in range(2):
            for e in range(experts_here):
                at = (kind * experts_here + e) * hidden_units
                left = cots[:, :, at:at + hidden_units].reshape(ranks * rows, hidden_units)
                total += contract(left, weights[kind, e, columns, :], ((1,), (1,)))
        total = total.astype(jnp.bfloat16)
        for r in range(ranks):
            x_buf[position(r, range(rank_bits)), :, columns] = total[r * rows:(r + 1) * rows]
        return 0

    order = list(range(rank_bits))
    token_job = Halving("expert", order, x_buf, c_buf, tok_send, tok_recv)
    score_job = Halving("expert", order, score, score_recv, score_send, score_recv_sem)
    outs = (gate_out, up_out, down_out)
    computed = {2}
    turn = 0
    for is_step, j, stage in events:
        job, kind, e, q = chunks[j]
        if kind not in computed:
            weight_grads(kind, x_buf)
            computed.add(kind)
            if len(computed) == 3:
                lax.fori_loop(0, width // (2 * LANES), token_part, 0)
                for bit in range(rank_bits):
                    pl.semaphore_wait(ready.at[bit], 1)
                token_job.start(0)
                score_job.start(0)
                turn = 0
        if not is_step:
            job.start(0)
            continue
        total = job.step(stage)
        if total is not None:
            outs[kind][e, q * part_rows:(q + 1) * part_rows, :] = total
        if len(computed) == 3 and turn % 4 == 3 and turn // 4 < rank_bits:
            total = token_job.step(turn // 4)
            if total is not None:
                tok_out[...] = total.astype(jnp.bfloat16)
            total = score_job.step(turn // 4)
            if total is not None:
                total = total.T
                for k in range(top):
                    picked = jnp.where(named[k], total, 0.0)
                    grads = jnp.sum(picked, axis=0, keepdims=True)
                    score_out[k:k + 1, :] = grads.astype(jnp.bfloat16)
        turn += 1
    for job in [chunk[0] for chunk in chunks] + [token_job, score_job]:
        job.finish()


def store(*refs):
    count = len(refs) // 2
    copies = [
        pltpu.make_async_copy(refs[i], refs[count + i], refs[-1].at[i]) for i in range(count)
    ]
    for copy in copies:
        copy.start()
    for copy in copies:
        copy.wait()


def local(ranks, groups, tokens, routes, combine, out_cotangent, gate_weight, up_weight, down_weight):
    rows, width = tokens.shape
    experts_here, _, hidden_units = gate_weight.shape
    owned = width // groups
    rank_bits, group_bits = ranks.bit_length() - 1, groups.bit_length() - 1
    bf16, dma = jnp.bfloat16, pltpu.SemaphoreType.DMA
    anywhere = pl.BlockSpec(memory_space=pl.ANY)
    vmem = pl.BlockSpec(memory_space=pltpu.VMEM)
    grad = jax.ShapeDtypeStruct((experts_here, owned, hidden_units), jnp.float32)
    chunk = (3, experts_here, PARTS)
    block = (owned // PARTS, hidden_units)
    results = pl.pallas_call(
        functools.partial(kernel, ranks, groups),
        out_shape=(
            jax.ShapeDtypeStruct((rows, width), bf16),
            jax.ShapeDtypeStruct(routes.shape[::-1], bf16),
            grad, grad, grad,
        ),
        in_specs=[vmem] * 2 + [anywhere] * 5,
        out_specs=(vmem,) * 5,
        scratch_shapes=[
            pltpu.VMEM((ranks, rows, width), bf16),
            pltpu.VMEM((ranks, rows, width), bf16),
            pltpu.VMEM((ranks, rows, LANES), bf16),
            pltpu.VMEM((2, experts_here, 2 * rows, hidden_units), jnp.float32),
            pltpu.VMEM((3,) + gate_weight.shape, bf16),
            pltpu.VMEM((ranks, rows, 3 * experts_here * hidden_units), bf16),
            pltpu.VMEM(chunk + (groups,) + block, bf16),
            pltpu.VMEM(chunk + (groups - 1,) + block, bf16),
            pltpu.VMEM((ranks, rows, LANES), bf16),
            pltpu.VMEM((ranks, rows, LANES), bf16),
            dma((5,)),
            dma((ranks, 3)),
            dma((ranks, 3)),
            dma(chunk + (group_bits,)),
            dma(chunk + (group_bits,)),
            dma((rank_bits,)),
            dma((rank_bits,)),
            dma((rank_bits,)),
            dma((rank_bits,)),
            pltpu.SemaphoreType.REGULAR((rank_bits,)),
        ],
        compiler_params=pltpu.CompilerParams(
            collective_id=0, has_side_effects=True, vmem_limit_bytes=62 * 2**20
        ),
    )(routes.T, combine.T, tokens, out_cotangent, gate_weight, up_weight, down_weight)
    results = pl.pallas_call(
        store,
        out_shape=tuple(jax.ShapeDtypeStruct(x.shape, x.dtype) for x in results),
        in_specs=[anywhere] * len(results),
        out_specs=(anywhere,) * len(results),
        scratch_shapes=[dma((len(results),))],
        compiler_params=pltpu.CompilerParams(vmem_limit_bytes=62 * 2**20),
    )(*results)
    token_grads, scores, gate_grads, up_grads, down_grads = results
    return token_grads, scores.T, gate_grads, up_grads, down_grads


def solution(mesh):
    ranks, groups = mesh.shape["expert"], mesh.shape["dp"]
    return jax.shard_map(
        functools.partial(local, ranks, groups),
        mesh=mesh,
        in_specs=(
            P(("dp", "expert"), None),
            P(("dp", "expert"), None),
            P(("dp", "expert"), None),
            P(("dp", "expert"), None),
            P("expert", None, None),
            P("expert", None, None),
            P("expert", None, None),
        ),
        out_specs=(
            P(("dp", "expert"), None),
            P(("dp", "expert"), None),
            P("expert", "dp", None),
            P("expert", "dp", None),
            P("expert", "dp", None),
        ),
        check_vma=False,
    )
```

```python
import functools

import jax
import jax.numpy as jnp
from jax import lax
from jax.experimental import pallas as pl
from jax.experimental.pallas import tpu as pltpu
from jax.sharding import PartitionSpec as P

MESH = pl.DeviceIdType.MESH
LANES = 128
PARTS = 4


def bit_of(index, bit):
    return (index // (1 << bit)) % 2


def flipped(index, bit):
    return index + (1 << bit) * (1 - 2 * bit_of(index, bit))


def partner_mask(index, mask, bits):
    for bit in range(bits):
        if mask >> bit & 1:
            index = flipped(index, bit)
    return index


def position(owner, order):
    place = 0
    for bit in order:
        place = place * 2 + bit_of(owner, bit)
    return place


class Halving:
    def __init__(self, axis, order, buf, recv, send_sem, recv_sem):
        self.axis, self.order, self.buf, self.recv = axis, order, buf, recv
        self.send_sem, self.recv_sem = send_sem, recv_sem
        self.me = lax.axis_index(axis)
        self.count = 1 << len(order)
        self.copies = []

    def base(self, stage):
        place = 0
        for step in range(stage):
            place = place + bit_of(self.me, self.order[step]) * (self.count >> (step + 1))
        return place

    def start(self, stage):
        size = self.count >> (stage + 1)
        bit = self.order[stage]
        begin = self.base(stage) + (1 - bit_of(self.me, bit)) * size
        offset = self.count - (self.count >> stage)
        copy = pltpu.make_async_remote_copy(
            src_ref=self.buf.at[pl.ds(begin, size)],
            dst_ref=self.recv.at[pl.ds(offset, size)],
            send_sem=self.send_sem.at[stage],
            recv_sem=self.recv_sem.at[stage],
            device_id={self.axis: flipped(self.me, bit)},
            device_id_type=MESH,
        )
        copy.start()
        self.copies.append(copy)

    def received(self, stage):
        self.copies[stage].wait_recv()
        size = self.count >> (stage + 1)
        begin = self.base(stage + 1)
        offset = self.count - (self.count >> stage)
        kept = self.buf[pl.ds(begin, size)].astype(jnp.float32)
        return begin, size, kept + self.recv[pl.ds(offset, size)].astype(jnp.float32)

    def step(self, stage):
        begin, size, total = self.received(stage)
        if stage == len(self.order) - 1:
            return total[0]
        self.buf[pl.ds(begin, size)] = total.astype(jnp.bfloat16)
        self.start(stage + 1)
        return None

    def finish(self):
        for copy in self.copies:
            copy.wait_send()


def plan(orders, blocks, links, depth):
    bits = len(orders[0])
    first_link = [links[order[0]] for order in orders]
    free = {link: 0.0 for link in links}
    waiting = {link: [j for j, at in enumerate(first_link) if at == link] for link in links}
    began = {link: [] for link in links}
    ready = []
    events = []
    while ready or any(waiting.values()):
        choices = [(max(free[links[orders[j][s]]], t), 0, t, j, s) for t, j, s in ready]
        choices += [(free[link], 1, 0.0, jobs[0], 0) for link, jobs in waiting.items() if jobs]
        begin, fresh, at, j, s = min(choices)
        link = links[orders[j][s]]
        end = begin + (blocks >> (s + 1))
        free[link] = end
        if fresh:
            waiting[link].pop(0)
            began[link].append(begin)
            back = len(began[link]) - depth
            events.append((began[link][back] if back >= 0 else -1.0, 0, j, 0))
        else:
            ready.remove((at, j, s))
        events.append((end, 1, j, s))
        if s + 1 < bits:
            ready.append((end, j, s + 1))
    return [event[1:] for event in sorted(events)]


def contract(left, right, dims):
    return lax.dot_general(left, right, (dims, ((), ())), preferred_element_type=jnp.float32)


def kernel(
    ranks, groups,
    routes_ref, combine_ref, tok_hbm, cot_hbm, gate_hbm, up_hbm, down_hbm,
    tok_out, score_out, gate_out, up_out, down_out,
    x_buf, c_buf, w_buf, acts, weights, cots, parts, parts_recv, score, score_recv,
    local_sem, gather_send, gather_recv, part_send, part_recv,
    tok_send, tok_recv, score_send, score_recv_sem, ready,
):
    rank_bits, group_bits = ranks.bit_length() - 1, groups.bit_length() - 1
    me, group = lax.axis_index("expert"), lax.axis_index("dp")
    experts_here, width, hidden_units = weights.shape[1:]
    rows = x_buf.shape[1]
    owned = width // groups
    part_rows = owned // PARTS

    loads = [
        pltpu.make_async_copy(src, weights.at[i], local_sem.at[i])
        for i, src in enumerate((gate_hbm, up_hbm, down_hbm))
    ]
    own = [
        pltpu.make_async_copy(src, dst.at[me], local_sem.at[3 + i])
        for i, (src, dst) in enumerate(((tok_hbm, x_buf), (cot_hbm, c_buf)))
    ]
    for copy in own + loads:
        copy.start()

    top = routes_ref.shape[0]
    expert = lax.broadcasted_iota(jnp.int32, (LANES, rows), 0)
    named = [expert == routes_ref[k:k + 1, :] for k in range(top)]
    dense = jnp.zeros((LANES, rows), jnp.float32)
    for k in range(top):
        dense = jnp.where(named[k], combine_ref[k:k + 1, :].astype(jnp.float32), dense)
    w_buf[me] = dense.T.astype(jnp.bfloat16)

    barrier = pltpu.get_barrier_semaphore()
    for bit in range(rank_bits):
        pl.semaphore_signal(barrier, 1, device_id={"expert": flipped(me, bit)}, device_id_type=MESH)
    for bit in range(group_bits):
        pl.semaphore_signal(barrier, 1, device_id={"dp": flipped(group, bit)}, device_id_type=MESH)
    pl.semaphore_wait(barrier, rank_bits + group_bits)

    gathered = {}

    def send_block(mask, bit, i):
        block = partner_mask(me, mask, rank_bits)
        dst = (x_buf, c_buf, w_buf)[i]
        slot = mask | 1 << bit
        copy = pltpu.make_async_remote_copy(
            src_ref=(tok_hbm, cot_hbm)[i] if mask == 0 and i < 2 else dst.at[block],
            dst_ref=dst.at[block],
            send_sem=gather_send.at[slot, i],
            recv_sem=gather_recv.at[slot, i],
            device_id={"expert": flipped(me, bit)},
            device_id_type=MESH,
        )
        copy.start()
        gathered[slot, i] = copy

    for bit in reversed(range(rank_bits)):
        send_block(0, bit, 2)
    for bit in reversed(range(rank_bits)):
        send_block(0, bit, 0)
    send_block(0, 0, 1)

    both = 2 * rows
    lane = lax.broadcasted_iota(jnp.int32, (both, LANES), 1)

    def forward(pair):
        x = x_buf[pl.ds(pair, 2)].reshape(both, width)
        for kind in range(2):
            for e in range(experts_here):
                acts[kind, e] = contract(x, weights[kind, e], ((1,), (0,)))

    def backward(pair):
        c = c_buf[pl.ds(pair, 2)].reshape(both, width)
        route_weights = w_buf[pl.ds(pair, 2)].reshape(both, LANES).astype(jnp.float32)
        scores = jnp.zeros((both, LANES), jnp.float32)
        for e in range(experts_here):
            mine = lane == me * experts_here + e
            weight = jnp.sum(jnp.where(mine, route_weights, 0.0), axis=1, keepdims=True)
            back = contract(c, weights[2, e], ((1,), (0,)))
            gate, up = acts[0, e], acts[1, e]
            sig = jax.nn.sigmoid(gate)
            act = gate * sig
            hidden = (act * up).astype(jnp.bfloat16).astype(jnp.float32)
            scores = jnp.where(mine, jnp.sum(back * hidden, axis=1, keepdims=True), scores)
            back = back * weight
            gate_cot = back * up * sig * (1.0 + gate * (1.0 - sig))
            for kind, value in enumerate((gate_cot, back * act, hidden * weight)):
                at = (kind * experts_here + e) * hidden_units
                value = value.astype(jnp.bfloat16).reshape(2, rows, hidden_units)
                cots[pl.ds(pair, 2), :, at:at + hidden_units] = value
        scores = scores.astype(jnp.bfloat16)
        for i in range(2):
            place = position(pair + i, range(rank_bits))
            score[place] = scores[i * rows:(i + 1) * rows]

    def arrived(mask, i):
        gathered[mask, i].wait_recv()
        lowest = (mask & -mask).bit_length() - 1
        for bit in reversed(range(lowest)):
            send_block(mask, bit, i)

    own_pair = me // 2 * 2
    own[0].wait()
    loads[0].wait()
    loads[1].wait()
    arrived(1, 0)
    forward(own_pair)
    own[1].wait()
    loads[2].wait()
    arrived(1, 1)
    arrived(1, 2)
    backward(own_pair)
    for bit in reversed(range(1, rank_bits)):
        gathered[1 << bit, 0].wait_send()
        send_block(0, bit, 1)
    for mask in range(2, ranks, 2):
        pair = partner_mask(own_pair, mask, rank_bits)
        for i in (2, 0):
            arrived(mask, i)
            arrived(mask + 1, i)
        forward(pair)
        arrived(mask, 1)
        arrived(mask + 1, 1)
        backward(pair)
    early = [(1 << bit, 0) for bit in range(1, rank_bits)]
    for key, copy in gathered.items():
        if key not in early:
            copy.wait_send()

    first = list(range(group_bits))
    second = [1, 0] + first[2:] if group_bits > 1 else first
    second_at = [(e, 0) for e in range(experts_here)]
    chunks = []
    for kind in (2, 0, 1):
        for e in range(experts_here):
            for q in range(PARTS):
                job = Halving(
                    "dp", second if (e, q) in second_at else first,
                    parts.at[kind, e, q], parts_recv.at[kind, e, q],
                    part_send.at[kind, e, q], part_recv.at[kind, e, q],
                )
                chunks.append((job, kind, e, q))
    links = [0 if bit < max(1, group_bits // 2) else 1 for bit in range(group_bits)]
    events = plan([chunk[0].order for chunk in chunks], groups, links, 3)

    def weight_grads(kind, source):
        at = kind * experts_here * hidden_units
        orders = {(e, q): job.order for job, kind_of, e, q in chunks if kind_of == kind}

        def one(owner, _):
            columns = pl.ds(pl.multiple_of(owner * owned, LANES), owned)
            left = source[:, :, columns].reshape(ranks * rows, owned)
            right = cots[:, :, at:at + experts_here * hidden_units]
            right = right.reshape(ranks * rows, experts_here * hidden_units)
            total = contract(left, right, ((0,), (0,))).astype(jnp.bfloat16)
            for e in range(experts_here):
                for q in range(PARTS):
                    parts[kind, e, q, position(owner, orders[e, q])] = total[
                        q * part_rows:(q + 1) * part_rows, e * hidden_units:(e + 1) * hidden_units
                    ]
            return 0

        lax.fori_loop(0, groups, one, 0)
    weight_grads(2, c_buf)
    early = [event for event in events if not event[0]][:6]
    early = [event for event in early if chunks[event[1]][1] == 2]
    for _, j, _ in early:
        chunks[j][0].start(0)
    for bit in range(rank_bits):
        pl.semaphore_signal(
            ready.at[bit], 1, device_id={"expert": flipped(me, bit)}, device_id_type=MESH
        )
    weight_grads(0, x_buf)
    weight_grads(1, x_buf)

    def token_part(step, _):
        strip = 2 * LANES
        columns = pl.ds(pl.multiple_of(step * strip, LANES), strip)
        total = jnp.zeros((ranks * rows, strip), jnp.float32)
        for kind in range(2):
            for e in range(experts_here):
                at = (kind * experts_here + e) * hidden_units
                left = cots[:, :, at:at + hidden_units].reshape(ranks * rows, hidden_units)
                total += contract(left, weights[kind, e, columns, :], ((1,), (1,)))
        total = total.astype(jnp.bfloat16)
        for r in range(ranks):
            x_buf[position(r, range(rank_bits)), :, columns] = total[r * rows:(r + 1) * rows]
        return 0

    lax.fori_loop(0, width // (2 * LANES), token_part, 0)
    order = list(range(rank_bits))
    token_job = Halving("expert", order, x_buf, c_buf, tok_send, tok_recv)
    score_job = Halving("expert", order, score, score_recv, score_send, score_recv_sem)
    for bit in range(rank_bits):
        pl.semaphore_wait(ready.at[bit], 1)
    token_job.start(0)
    score_job.start(0)

    outs = (gate_out, up_out, down_out)
    turn = 0
    for event in events:
        is_step, j, stage = event
        job, kind, e, q = chunks[j]
        if not is_step:
            if event not in early:
                job.start(0)
            continue
        total = job.step(stage)
        if total is not None:
            outs[kind][e, q * part_rows:(q + 1) * part_rows, :] = total
        if turn % 8 == 7 and turn // 8 < rank_bits:
            total = token_job.step(turn // 8)
            if total is not None:
                tok_out[...] = total.astype(jnp.bfloat16)
            total = score_job.step(turn // 8)
            if total is not None:
                total = total.T
                for k in range(top):
                    picked = jnp.where(named[k], total, 0.0)
                    grads = jnp.sum(picked, axis=0, keepdims=True)
                    score_out[k:k + 1, :] = grads.astype(jnp.bfloat16)
        turn += 1
    for job in [chunk[0] for chunk in chunks] + [token_job, score_job]:
        job.finish()


def store(*refs):
    count = len(refs) // 2
    copies = [
        pltpu.make_async_copy(refs[i], refs[count + i], refs[-1].at[i]) for i in range(count)
    ]
    for copy in copies:
        copy.start()
    for copy in copies:
        copy.wait()


def local(ranks, groups, tokens, routes, combine, out_cotangent, gate_weight, up_weight, down_weight):
    rows, width = tokens.shape
    experts_here, _, hidden_units = gate_weight.shape
    owned = width // groups
    rank_bits, group_bits = ranks.bit_length() - 1, groups.bit_length() - 1
    bf16, dma = jnp.bfloat16, pltpu.SemaphoreType.DMA
    anywhere = pl.BlockSpec(memory_space=pl.ANY)
    vmem = pl.BlockSpec(memory_space=pltpu.VMEM)
    grad = jax.ShapeDtypeStruct((experts_here, owned, hidden_units), jnp.float32)
    chunk = (3, experts_here, PARTS)
    block = (owned // PARTS, hidden_units)
    results = pl.pallas_call(
        functools.partial(kernel, ranks, groups),
        out_shape=(
            jax.ShapeDtypeStruct((rows, width), bf16),
            jax.ShapeDtypeStruct(routes.shape[::-1], bf16),
            grad, grad, grad,
        ),
        in_specs=[vmem] * 2 + [anywhere] * 5,
        out_specs=(vmem,) * 5,
        scratch_shapes=[
            pltpu.VMEM((ranks, rows, width), bf16),
            pltpu.VMEM((ranks, rows, width), bf16),
            pltpu.VMEM((ranks, rows, LANES), bf16),
            pltpu.VMEM((2, experts_here, 2 * rows, hidden_units), jnp.float32),
            pltpu.VMEM((3,) + gate_weight.shape, bf16),
            pltpu.VMEM((ranks, rows, 3 * experts_here * hidden_units), bf16),
            pltpu.VMEM(chunk + (groups,) + block, bf16),
            pltpu.VMEM(chunk + (groups - 1,) + block, bf16),
            pltpu.VMEM((ranks, rows, LANES), bf16),
            pltpu.VMEM((ranks, rows, LANES), bf16),
            dma((5,)),
            dma((ranks, 3)),
            dma((ranks, 3)),
            dma(chunk + (group_bits,)),
            dma(chunk + (group_bits,)),
            dma((rank_bits,)),
            dma((rank_bits,)),
            dma((rank_bits,)),
            dma((rank_bits,)),
            pltpu.SemaphoreType.REGULAR((rank_bits,)),
        ],
        compiler_params=pltpu.CompilerParams(
            collective_id=0, has_side_effects=True, vmem_limit_bytes=62 * 2**20
        ),
    )(routes.T, combine.T, tokens, out_cotangent, gate_weight, up_weight, down_weight)
    results = pl.pallas_call(
        store,
        out_shape=tuple(jax.ShapeDtypeStruct(x.shape, x.dtype) for x in results),
        in_specs=[vmem] * len(results),
        out_specs=(anywhere,) * len(results),
        scratch_shapes=[dma((len(results),))],
    )(*results)
    token_grads, scores, gate_grads, up_grads, down_grads = results
    return token_grads, scores.T, gate_grads, up_grads, down_grads


def solution(mesh):
    ranks, groups = mesh.shape["expert"], mesh.shape["dp"]
    return jax.shard_map(
        functools.partial(local, ranks, groups),
        mesh=mesh,
        in_specs=(
            P(("dp", "expert"), None),
            P(("dp", "expert"), None),
            P(("dp", "expert"), None),
            P(("dp", "expert"), None),
            P("expert", None, None),
            P("expert", None, None),
            P("expert", None, None),
        ),
        out_specs=(
            P(("dp", "expert"), None),
            P(("dp", "expert"), None),
            P("expert", "dp", None),
            P("expert", "dp", None),
            P("expert", "dp", None),
        ),
        check_vma=False,
    )
```
